32 devices in a mesh: expert: 16 (over z, y, x), replica: 2 (over core).
Axes of the slice: x: 2, y: 2, z: 4, core: 2. Of those that a mesh axis runs over, the one named last changes fastest.
Arguments:
- x_quant: bfloat16 [4096, 2048], P(('expert', 'replica')), may hold values from -6 to 6
- x_scale: float32 [4096, 16], P(('expert', 'replica')), may hold values from 0.3 to 3
- out_grad: bfloat16 [4096, 2048], P(('expert', 'replica')), may hold values from -6 to 6
- expert_ids: int32 [4096, 8], P(('expert', 'replica')), may hold values from 0 to 15, all different within a row; in each aligned block of 128 rows (0 to 127, 128 to 255, ...) at most 80 rows name the same one
- gate_fixed: int32 [4096, 8], P(('expert', 'replica')), may hold values from 1024 to 16383
- w_gate: bfloat16 [16, 2048, 768], P('expert'), may hold values from -0.125 to 0.125
- s_gate: float32 [16, 16, 6], P('expert'), may hold values from 0.3 to 3
- w_up: bfloat16 [16, 2048, 768], P('expert'), may hold values from -0.125 to 0.125
- s_up: float32 [16, 16, 6], P('expert'), may hold values from 0.3 to 3
- w_down: bfloat16 [16, 768, 2048], P('expert'), may hold values from -0.21875 to 0.21875
- s_down: float32 [16, 6, 16], P('expert'), may hold values from 0.3 to 3
Outputs:
- grad_input: bfloat16 [4096, 2048], P(('expert', 'replica'))
- grad_gate: bfloat16 [16, 2048, 768], P('expert', None, 'replica')
- grad_up: bfloat16 [16, 2048, 768], P('expert', None, 'replica')
- grad_down: bfloat16 [16, 768, 2048], P('expert', 'replica')
The draws below stay inside these ranges and needn't reach their ends.
Inputs may be any that keep to these rules, and one draw needn't show every extreme that they name: `expert_ids`: each row names 8 different experts. Among the rows of one device at most 80 name the same expert, and in every draw some expert is named by exactly 80 rows of some device.
All inputs are finite; a program needn't handle non-finite values.
Results may differ from the reference program's by a relative error of at most 0.012.
Values may be sent and summed in bfloat16 or wider, within the bound.
A program may use at most 192 MiB of HBM per device.

```python
import math
import jax
import jax.numpy as jnp
import numpy as np
from jax import lax

D = 2048
FF = 768
TOPK = 8
BLK = 128
TOK_DEV = 128
EXPERTS = 16
CAP = 80
TOKENS = 4096


def plant(result, stream_key, low, high):
    dims = result.shape
    index_at = [jax.random.randint(jax.random.fold_in(stream_key, axis), (), 0, dims[axis]) for axis in range(len(dims))]
    result = result.at[tuple(index_at)].set(low)
    longest = dims.index(max(dims))
    index_at[longest] = (index_at[longest] + 1) % dims[longest]
    return result.at[tuple(index_at)].set(high)


def steps_of(key, dims, cuts, least, top_value):
    loudness = 1.0
    for position, blocks in cuts:
        draws = jax.random.uniform(jax.random.fold_in(jax.random.fold_in(key, 6), position), (blocks,), jnp.float32, least / len(cuts), top_value / len(cuts))
        loudness = loudness * jnp.repeat(jnp.exp(draws), dims[position] // blocks).reshape((-1,) + (1,) * (len(dims) - 1 - position))
    return loudness


def assign_block(key, own, number, rows, number_of, top, bound, lean):
    order = jax.random.permutation(key, number_of)
    crowded, ordinary = portions_of(number_of, rows * top, bound, lean, True), portions_of(number_of, rows * top, bound, lean, False)
    places = jnp.arange(number_of)

    def named(tallies, turn):
        used = int((tallies > 0).sum())
        fixed = max(1, used // 4)
        passed = fixed + (places - fixed + turn * (used - fixed)) % max(1, number_of - fixed)
        return jnp.zeros((number_of,), jnp.int32).at[order[jnp.where(places < fixed, places, passed)]].set(jnp.asarray(tallies, jnp.int32))

    tallies = jnp.where(number % 4 == 0, named(crowded, number // 4), named(ordinary, number - number // 4 - 1))
    mixed = jax.random.permutation(jax.random.fold_in(own, 3), number_of)
    donor, taker = mixed[0:number_of // 2 * 2:2], mixed[1:number_of // 2 * 2:2]
    margin = jnp.minimum(tallies[donor] - 1, bound - tallies[taker]) // 2
    margin = jnp.where((donor == order[0]) | (taker == order[0]) | (tallies[taker] == 0), 0, jnp.maximum(margin, 0))
    passed = jax.random.randint(jax.random.fold_in(own, 4), (number_of // 2,), 0, 1 << 20) % (margin + 1)
    tallies = tallies.at[donor].add(-passed).at[taker].add(passed)
    items = jnp.searchsorted(jnp.cumsum(tallies), jnp.arange(rows * top), side="right").astype(jnp.int32)
    table = items.reshape(top, rows).T
    table = table[jax.random.permutation(jax.random.fold_in(own, 1), rows)]
    turn = jax.random.randint(jax.random.fold_in(own, 2), (rows, 1), 0, top)
    return jnp.take_along_axis(table, (jnp.arange(top)[None, :] + turn) % top, axis=1)


def portions_of(amount, total, most, lean, full):
    weights = [(1 << 20) // math.isqrt(rank ** lean) + 1 for rank in range(1, amount + 1)]
    largest = most if full else min(most, max(-(-total // amount), total * weights[0] // sum(weights)))
    least = 1 if total - largest >= amount - 1 else 0
    holding, surplus = [largest] + [least] * (amount - 1), total - largest - least * (amount - 1)
    while surplus > 0:
        movable = [i for i in range(1, amount) if holding[i] < largest] or [i for i in range(1, amount) if holding[i] < most]
        whole, budget = sum([weights[i] for i in movable]), surplus
        for i in movable:
            more = min(most - holding[i], max(1, budget * weights[i] // whole), surplus)
            holding[i] = holding[i] + more
            surplus = surplus - more
    return np.array(holding)


def noise(stream_key, extent, width, bound, split=(), kind=jnp.bfloat16):
    entries = jax.random.normal(stream_key, extent, jnp.float32) * width
    if len(split) > 0:
        entries = steps_of(stream_key, extent, split, -0.22, 0.18) * entries
    return jnp.clip(entries, min=-bound, max=bound).astype(kind)


def setup_inputs(seed: int = 0) -> dict:
    keys = jax.random.split(jax.random.key(seed), 12)
    x_quant = noise(keys[0], (TOKENS, D), 1.0, 6.0, ((0, 32),))
    x_scale = jnp.clip(jnp.exp(math.log(3.0) - 2.3025851 * jax.random.uniform(keys[1], (TOKENS, D // BLK), jnp.float32) ** steps_of(keys[1], (TOKENS, D // BLK), ((0, 32),), -0.2, 0.2)), 0.3, 3.0)
    out_grad = noise(keys[2], (TOKENS, D), 1.0, 6.0, ((0, 32),))
    expert_ids_keys = jax.random.split(jax.random.fold_in(keys[3], 1), TOKENS // TOK_DEV)
    expert_ids_turns = jax.random.permutation(jax.random.fold_in(keys[3], 3), TOKENS // TOK_DEV)
    expert_ids = jax.vmap(lambda own, number: assign_block(jax.random.fold_in(keys[3], 2), own, number, TOK_DEV, EXPERTS, TOPK, CAP, 2))(expert_ids_keys, expert_ids_turns).reshape((TOKENS, TOPK))
    gate_fixed = plant(jax.random.randint(keys[4], (TOKENS, TOPK), 1024, 16384), jax.random.fold_in(keys[4], 1), 1024, 16383).astype(jnp.int32)
    w_gate = noise(keys[5], (EXPERTS, D, FF), D ** -0.5, 0.125, ((0, 16),))
    s_gate = jnp.clip(jnp.exp(math.log(3.0) - 2.3025851 * jax.random.uniform(keys[6], (EXPERTS, D // BLK, FF // BLK), jnp.float32) ** steps_of(keys[6], (EXPERTS, D // BLK, FF // BLK), ((0, 16),), -0.2, 0.2)), 0.3, 3.0)
    w_up = noise(keys[7], (EXPERTS, D, FF), D ** -0.5, 0.125, ((0, 16),))
    s_up = jnp.clip(jnp.exp(math.log(3.0) - 2.3025851 * jax.random.uniform(keys[8], (EXPERTS, D // BLK, FF // BLK), jnp.float32) ** steps_of(keys[8], (EXPERTS, D // BLK, FF // BLK), ((0, 16),), -0.2, 0.2)), 0.3, 3.0)
    w_down = noise(keys[9], (EXPERTS, FF, D), FF ** -0.5, 0.21875, ((0, 16),))
    s_down = jnp.clip(jnp.exp(math.log(3.0) - 2.3025851 * jax.random.uniform(keys[10], (EXPERTS, FF // BLK, D // BLK), jnp.float32) ** steps_of(keys[10], (EXPERTS, FF // BLK, D // BLK), ((0, 16),), -0.2, 0.2)), 0.3, 3.0)
    return {"x_quant": x_quant, "x_scale": x_scale, "out_grad": out_grad, "expert_ids": expert_ids, "gate_fixed": gate_fixed, "w_gate": w_gate, "s_gate": s_gate, "w_up": w_up, "s_up": s_up, "w_down": w_down, "s_down": s_down}


def dequant(weight, scale):
    rows, cols = weight.shape
    srows, scols = scale.shape
    blocks = weight.reshape(srows, rows // srows, scols, cols // scols).astype(jnp.float32)
    return (blocks * scale[:, None, :, None]).reshape(rows, cols).astype(jnp.bfloat16)


def block_slots(flat_ids):
    onehot = (flat_ids[:, None] == jnp.arange(EXPERTS, dtype=jnp.int32)[None, :]).astype(jnp.int32)
    before = jnp.cumsum(onehot, axis=0) - onehot
    return jnp.sum(before * onehot, axis=1).astype(jnp.int32)


def reference(x_quant, x_scale, out_grad, expert_ids, gate_fixed, w_gate, s_gate, w_up, s_up, w_down, s_down):
    blocks_count = TOKENS // TOK_DEV
    scaled = x_quant.reshape(TOKENS, D // BLK, BLK).astype(jnp.float32) * x_scale[:, :, None]
    inputs = scaled.reshape(TOKENS, D).astype(jnp.bfloat16)
    flat = expert_ids.reshape(blocks_count, TOK_DEV * TOPK).astype(jnp.int32)
    slots = jax.vmap(block_slots)(flat)
    within = (jnp.arange(TOK_DEV * TOPK, dtype=jnp.int32) // TOPK)[None, :]
    owners = jnp.arange(blocks_count, dtype=jnp.int32)[:, None]
    token_index = (owners * TOK_DEV + within).astype(jnp.int32)
    owner_full = jnp.broadcast_to(owners, flat.shape)
    table = jnp.full((EXPERTS, blocks_count, CAP), TOKENS, jnp.int32).at[flat, owner_full, slots].set(token_index)
    gate_vals = gate_fixed.reshape(blocks_count, TOK_DEV * TOPK).astype(jnp.float32) / 65536.0
    gate_table = jnp.zeros((EXPERTS, blocks_count, CAP), jnp.float32).at[flat, owner_full, slots].set(gate_vals)
    input_pad = jnp.concatenate([inputs, jnp.zeros((1, D), jnp.bfloat16)], axis=0)
    grad_pad = jnp.concatenate([out_grad, jnp.zeros((1, D), jnp.bfloat16)], axis=0)

    def one_expert(total, packed):
        index, gates, wg, sg, wu, su, wd, sd = packed
        rows = index.reshape(-1)
        gate_w = dequant(wg, sg)
        up_w = dequant(wu, su)
        down_w = dequant(wd, sd)
        xrows = input_pad[rows]
        row_grad = (gates.reshape(-1)[:, None] * grad_pad[rows].astype(jnp.float32)).astype(jnp.bfloat16)
        pre_gate = jnp.dot(xrows, gate_w, preferred_element_type=jnp.float32)
        pre_up = jnp.dot(xrows, up_w, preferred_element_type=jnp.float32)
        sig = jax.nn.sigmoid(pre_gate)
        act = pre_gate * sig
        hidden = (act * pre_up).astype(jnp.bfloat16)
        hidden_grad = jnp.dot(row_grad, down_w.T, preferred_element_type=jnp.float32)
        up_grad = (hidden_grad * act).astype(jnp.bfloat16)
        gate_grad = (hidden_grad * pre_up * sig * (1.0 + pre_gate * (1.0 - sig))).astype(jnp.bfloat16)
        row_input = jnp.dot(gate_grad, gate_w.T, preferred_element_type=jnp.float32)
        row_input = row_input + jnp.dot(up_grad, up_w.T, preferred_element_type=jnp.float32)
        row_input = lax.optimization_barrier(row_input.astype(jnp.bfloat16)).astype(jnp.float32)
        total = total.at[rows].add(row_input)
        grad_g = jnp.dot(xrows.T, gate_grad, preferred_element_type=jnp.float32).astype(jnp.bfloat16)
        grad_u = jnp.dot(xrows.T, up_grad, preferred_element_type=jnp.float32).astype(jnp.bfloat16)
        grad_d = jnp.dot(hidden.T, row_grad, preferred_element_type=jnp.float32).astype(jnp.bfloat16)
        return total, (grad_g, grad_u, grad_d)

    start = jnp.zeros((TOKENS + 1, D), jnp.float32)
    total, (grad_gate, grad_up, grad_down) = lax.scan(one_expert, start, (table, gate_table, w_gate, s_gate, w_up, s_up, w_down, s_down))
    return total[:TOKENS].astype(jnp.bfloat16), grad_gate, grad_up, grad_down
```

```python
import jax
import jax.numpy as jnp
from jax import lax
from jax.sharding import PartitionSpec as P


def dequant(weight, scale):
    rows, cols = weight.shape
    srows, scols = scale.shape
    blocks = weight.reshape(srows, rows // srows, scols, cols // scols).astype(jnp.float32)
    return (blocks * scale[:, None, :, None]).reshape(rows, cols).astype(jnp.bfloat16)


def shards(
    x_quant, x_scale, out_grad, expert_ids, gate_fixed, w_gate, s_gate, w_up, s_up, w_down, s_down
):
    f32, bf16 = jnp.float32, jnp.bfloat16
    tok_rows, width = x_quant.shape
    topk = expert_ids.shape[1]
    experts = lax.axis_size("expert")
    capacity = tok_rows * topk * 5 // (4 * experts)
    blk_width = width // x_scale.shape[1]
    scaled = x_quant.reshape(tok_rows, -1, blk_width).astype(f32) * x_scale[:, :, None]
    inputs = scaled.reshape(tok_rows, width).astype(bf16)
    named = expert_ids[None, :, :] == jnp.arange(experts, dtype=jnp.int32)[:, None, None]
    units = jnp.sum(jnp.where(named, gate_fixed[None], 0), axis=2).astype(f32)
    units = lax.all_to_all(units, "expert", split_axis=0, concat_axis=0, tiled=True)
    all_x = lax.all_gather(inputs, "expert", axis=0, tiled=False)
    all_g = lax.all_gather(out_grad, "expert", axis=0, tiled=False)

    chosen = units > 0
    rank = jnp.cumsum(chosen.astype(jnp.int32), axis=1) - 1
    pick = chosen[:, None, :] & (
        rank[:, None, :] == jnp.arange(capacity, dtype=jnp.int32)[None, :, None]
    )
    gates = jnp.sum(jnp.where(pick, units[:, None, :], 0.0), axis=2) / 65536.0
    pick = pick.astype(bf16)

    gate_w = dequant(w_gate[0], s_gate[0])
    up_w = dequant(w_up[0], s_up[0])
    down_w = dequant(w_down[0], s_down[0])
    rows = experts * capacity
    xrows = jnp.einsum("ect,etd->ecd", pick, all_x, preferred_element_type=f32)
    xrows = xrows.astype(bf16).reshape(rows, width)
    row_grad = jnp.einsum("ect,etd->ecd", pick, all_g, preferred_element_type=f32)
    row_grad = (row_grad * gates[:, :, None]).astype(bf16).reshape(rows, width)
    pre_gate = jnp.dot(xrows, gate_w, preferred_element_type=f32)
    pre_up = jnp.dot(xrows, up_w, preferred_element_type=f32)
    sig = jax.nn.sigmoid(pre_gate)
    act = pre_gate * sig
    hidden = (act * pre_up).astype(bf16)
    hidden_grad = jnp.dot(row_grad, down_w.T, preferred_element_type=f32)
    up_grad = (hidden_grad * act).astype(bf16)
    gate_grad = (hidden_grad * pre_up * sig * (1.0 + pre_gate * (1.0 - sig))).astype(bf16)
    row_input = jnp.dot(gate_grad, gate_w.T, preferred_element_type=f32)
    row_input = row_input + jnp.dot(up_grad, up_w.T, preferred_element_type=f32)
    back = row_input.astype(bf16).reshape(experts, capacity, width)
    spread = jnp.einsum("ect,ecd->etd", pick, back, preferred_element_type=f32).astype(bf16)
    grad_input = lax.psum_scatter(
        spread.reshape(experts * tok_rows, width), "expert", scatter_dimension=0, tiled=True
    )
    term_gate = jnp.dot(xrows.T, gate_grad, preferred_element_type=f32).astype(bf16)
    term_up = jnp.dot(xrows.T, up_grad, preferred_element_type=f32).astype(bf16)
    term_down = jnp.dot(hidden.T, row_grad, preferred_element_type=f32).astype(bf16)
    sum_gate = lax.psum_scatter(term_gate, "replica", scatter_dimension=1, tiled=True)
    sum_up = lax.psum_scatter(term_up, "replica", scatter_dimension=1, tiled=True)
    sum_down = lax.psum_scatter(term_down, "replica", scatter_dimension=0, tiled=True)
    return (grad_input, sum_gate[None], sum_up[None], sum_down[None])


def solution(mesh):
    tokens = P(("expert", "replica"), None)
    weights = P("expert", None, None)
    return jax.shard_map(
        shards,
        mesh=mesh,
        in_specs=(tokens,) * 5 + (weights,) * 6,
        out_specs=(
            tokens,
            P("expert", None, "replica"),
            P("expert", None, "replica"),
            P("expert", "replica", None),
        ),
        check_vma=False,
    )
```

```python
import jax
import jax.numpy as jnp
from jax import lax
from jax.experimental import pallas as pl
from jax.experimental.pallas import tpu as pltpu
from jax.sharding import PartitionSpec as P

DEPTH = 4


def place():
    me = lax.axis_index("expert")
    z, q = me // 4, me % 4
    x, y = q % 2, q // 2
    return me, z, q, q + 1 - 2 * x, q + 2 - 4 * y, 3 - q


def greet(me, z, qx, qy):
    barrier = pltpu.get_barrier_semaphore()
    for dev in (4 * z + qx, 4 * z + qy):
        pl.semaphore_signal(barrier, inc=1, device_id={"expert": dev})

    @pl.when(z > 0)
    def _():
        pl.semaphore_signal(barrier, inc=1, device_id={"expert": me - 4})

    @pl.when(z < DEPTH - 1)
    def _():
        pl.semaphore_signal(barrier, inc=1, device_id={"expert": me + 4})

    peers = 2 + jnp.minimum(z, 1) + jnp.minimum(DEPTH - 1 - z, 1)
    pl.semaphore_wait(barrier, peers)


def gather_kernel(x_ref, g_ref, all_x, all_g, send_sem, recv_sem, own_sem):
    me, z, q, qx, qy, qd = place()
    full, own = (all_x, all_g), (x_ref, g_ref)
    greet(me, z, qx, qy)

    def at_depth(zz):
        sent = []

        def send(a, block, way, mine=False):
            dev = (4 * zz + qx, 4 * zz + qy, me + 4, me - 4)[way]
            copy = pltpu.make_async_remote_copy(
                src_ref=own[a] if mine else full[a].at[block],
                dst_ref=full[a].at[block],
                send_sem=send_sem.at[a, block, way],
                recv_sem=recv_sem.at[a, block],
                device_id={"expert": dev},
            )
            copy.start()
            sent.append(copy)

        def arrive(a, block):
            pltpu.make_async_remote_copy(
                src_ref=full[a].at[block],
                dst_ref=full[a].at[block],
                send_sem=send_sem.at[a, block, 0],
                recv_sem=recv_sem.at[a, block],
                device_id={"expert": 4 * zz + qx},
            ).wait_recv()

        def column(src):
            for a in range(2):
                if src != zz:
                    arrive(a, 4 * src + q)
                if src <= zz < DEPTH - 1:
                    send(a, 4 * src + q, 2, src == zz)
                if src >= zz > 0:
                    send(a, 4 * src + q, 3, src == zz)
                send(a, 4 * src + q, 0, src == zz)
                send(a, 4 * src + q, 1, src == zz)

        def relay(src):
            arrive(1, 4 * src + qx)
            send(1, 4 * src + qx, 1)
            arrive(0, 4 * src + qy)
            send(0, 4 * src + qy, 0)

        order = sorted(range(DEPTH), key=lambda s: (abs(s - zz), s))
        column(order[0])
        kept = [pltpu.make_async_copy(own[a], full[a].at[me], own_sem.at[a]) for a in range(2)]
        for copy in kept:
            copy.start()
        for i in range(DEPTH):
            if i + 1 < DEPTH:
                column(order[i + 1])
            relay(order[i])
        for src in order:
            arrive(0, 4 * src + qx)
            arrive(1, 4 * src + qy)
            arrive(0, 4 * src + qd)
            arrive(1, 4 * src + qd)
        for copy in kept:
            copy.wait()
        for copy in sent:
            copy.wait_send()

    for zz in range(DEPTH):
        pl.when(z == zz)(lambda zz=zz: at_depth(zz))


def gather_tokens(inputs, out_grad):
    shape = jax.ShapeDtypeStruct((4 * DEPTH, *inputs.shape), inputs.dtype)
    return pl.pallas_call(
        gather_kernel,
        out_shape=(shape, shape),
        in_specs=[pl.BlockSpec(memory_space=pl.ANY)] * 2,
        out_specs=(pl.BlockSpec(memory_space=pl.ANY),) * 2,
        scratch_shapes=[
            pltpu.SemaphoreType.DMA((2, 4 * DEPTH, 4)),
            pltpu.SemaphoreType.DMA((2, 4 * DEPTH)),
            pltpu.SemaphoreType.DMA((2,)),
        ],
        compiler_params=pltpu.CompilerParams(collective_id=0, has_side_effects=True),
    )(inputs, out_grad)


def scatter_kernel(
    part, out, halves, far, near, column, above, send_sem, far_sem, near_sem, above_sem
):
    me, z, q, qx, qy, qd = place()
    rows, width = out.shape
    half = width // 2
    cut = (pl.ds(0, half), pl.ds(half, half))
    step = 16
    greet(me, z, qx, qy)

    def total(dst, terms):
        def body(i, carry):
            at = pl.ds(pl.multiple_of(i * step, step), step)
            acc = terms[0][at, :].astype(jnp.float32)
            for term in terms[1:]:
                acc = acc + term[at, :].astype(jnp.float32)
            dst[at, :] = acc.astype(dst.dtype)
            return carry

        lax.fori_loop(0, rows // step, body, 0)

    def at_depth(zz):
        sent = []
        plane = (4 * zz + qx, 4 * zz + qy)

        def send(src_ref, dst_ref, sem, recv, dev):
            copy = pltpu.make_async_remote_copy(
                src_ref=src_ref,
                dst_ref=dst_ref,
                send_sem=sem,
                recv_sem=recv,
                device_id={"expert": dev},
            )
            copy.start()
            sent.append(copy)

        def arrive(ref, recv):
            pltpu.make_async_remote_copy(
                src_ref=ref,
                dst_ref=ref,
                send_sem=send_sem.at[0, 0],
                recv_sem=recv,
                device_id={"expert": plane[0]},
            ).wait_recv()

        def first(s):
            for h in (0, 1):
                send(
                    part.at[4 * s + qd, :, cut[h]],
                    far.at[h, s],
                    send_sem.at[s, h],
                    far_sem.at[h, s],
                    plane[1 - h],
                )
            for way, block in ((0, 4 * s + qx), (1, 4 * s + qy)):
                h = 1 - way
                send(
                    part.at[block, :, cut[h]],
                    near.at[way, h, s],
                    send_sem.at[s, 2 + way],
                    near_sem.at[way, h, s],
                    plane[way],
                )

        def second(s):
            for way, block in ((0, 4 * s + qx), (1, 4 * s + qy)):
                h = way
                arrive(far.at[h, s], far_sem.at[h, s])
                total(halves.at[way, s], [part.at[block, :, cut[h]], far.at[h, s]])
                send(
                    halves.at[way, s],
                    near.at[way, h, s],
                    send_sem.at[s, 4 + way],
                    near_sem.at[way, h, s],
                    plane[way],
                )

        def third(s):
            slots = []
            if s <= zz < DEPTH - 1:
                slots.append(s)
            if s >= zz > 0:
                slots.append(DEPTH if s == zz else s)
            for way in (0, 1):
                for h in (0, 1):
                    arrive(near.at[way, h, s], near_sem.at[way, h, s])
            for slot in slots:
                arrive(above.at[slot], above_sem.at[slot])
            dst = out if s == zz else column.at[s]
            for h in (0, 1):
                terms = [part.at[4 * s + q, :, cut[h]], near.at[0, h, s], near.at[1, h, s]]
                terms += [above.at[slot, :, cut[h]] for slot in slots]
                total(dst.at[:, cut[h]], terms)
            if s != zz:
                nxt = zz - 1 if s < zz else zz + 1
                slot = DEPTH if s > zz and nxt == s else s
                send(
                    column.at[s],
                    above.at[slot],
                    send_sem.at[s, 6],
                    above_sem.at[slot],
                    me - 4 if s < zz else me + 4,
                )

        order = sorted(range(DEPTH), key=lambda s: (-abs(s - zz), s))
        for i in range(DEPTH + 2):
            if i < DEPTH:
                first(order[i])
            if 0 <= i - 1 < DEPTH:
                second(order[i - 1])
            if 0 <= i - 2 < DEPTH:
                third(order[i - 2])
        for copy in sent:
            copy.wait_send()

    for zz in range(DEPTH):
        pl.when(z == zz)(lambda zz=zz: at_depth(zz))


def scatter_sums(part):
    blocks, rows, width = part.shape
    half = width // 2
    dtype = part.dtype
    return pl.pallas_call(
        scatter_kernel,
        out_shape=jax.ShapeDtypeStruct((rows, width), dtype),
        in_specs=[pl.BlockSpec(memory_space=pltpu.VMEM)],
        out_specs=pl.BlockSpec(memory_space=pltpu.VMEM),
        scratch_shapes=[
            pltpu.VMEM((2, DEPTH, rows, half), dtype),
            pltpu.VMEM((2, DEPTH, rows, half), dtype),
            pltpu.VMEM((2, 2, DEPTH, rows, half), dtype),
            pltpu.VMEM((DEPTH, rows, width), dtype),
            pltpu.VMEM((DEPTH + 1, rows, width), dtype),
            pltpu.SemaphoreType.DMA((DEPTH, 7)),
            pltpu.SemaphoreType.DMA((2, DEPTH)),
            pltpu.SemaphoreType.DMA((2, 2, DEPTH)),
            pltpu.SemaphoreType.DMA((DEPTH + 1,)),
        ],
        compiler_params=pltpu.CompilerParams(
            collective_id=1, has_side_effects=True, vmem_limit_bytes=40 * 1024 * 1024
        ),
    )(part)


def dequant(weight, scale):
    rows, cols = weight.shape
    srows, scols = scale.shape
    blocks = weight.reshape(srows, rows // srows, scols, cols // scols).astype(jnp.float32)
    return (blocks * scale[:, None, :, None]).reshape(rows, cols).astype(jnp.bfloat16)


def shards(
    x_quant, x_scale, out_grad, expert_ids, gate_fixed, w_gate, s_gate, w_up, s_up, w_down, s_down
):
    f32, bf16 = jnp.float32, jnp.bfloat16
    tok_rows, width = x_quant.shape
    topk = expert_ids.shape[1]
    experts = lax.axis_size("expert")
    capacity = tok_rows * topk * 5 // (4 * experts)
    blk_width = width // x_scale.shape[1]
    scaled = x_quant.reshape(tok_rows, -1, blk_width).astype(f32) * x_scale[:, :, None]
    inputs = scaled.reshape(tok_rows, width).astype(bf16)
    named = expert_ids[None, :, :] == jnp.arange(experts, dtype=jnp.int32)[:, None, None]
    units = jnp.sum(jnp.where(named, gate_fixed[None], 0), axis=2).astype(f32)
    units = lax.all_to_all(units, "expert", split_axis=0, concat_axis=0, tiled=True)
    if experts == 4 * DEPTH:
        all_x, all_g = gather_tokens(inputs, out_grad)
    else:
        all_x = lax.all_gather(inputs, "expert", axis=0, tiled=False)
        all_g = lax.all_gather(out_grad, "expert", axis=0, tiled=False)

    chosen = units > 0
    rank = jnp.cumsum(chosen.astype(jnp.int32), axis=1) - 1
    pick = chosen[:, None, :] & (
        rank[:, None, :] == jnp.arange(capacity, dtype=jnp.int32)[None, :, None]
    )
    gates = jnp.sum(jnp.where(pick, units[:, None, :], 0.0), axis=2) / 65536.0
    pick = pick.astype(bf16)

    gate_w = dequant(w_gate[0], s_gate[0])
    up_w = dequant(w_up[0], s_up[0])
    down_w = dequant(w_down[0], s_down[0])
    rows = experts * capacity
    xrows = jnp.einsum("ect,etd->ecd", pick, all_x, preferred_element_type=f32)
    xrows = xrows.astype(bf16).reshape(rows, width)
    row_grad = jnp.einsum("ect,etd->ecd", pick, all_g, preferred_element_type=f32)
    row_grad = (row_grad * gates[:, :, None]).astype(bf16).reshape(rows, width)
    pre_gate = jnp.dot(xrows, gate_w, preferred_element_type=f32)
    pre_up = jnp.dot(xrows, up_w, preferred_element_type=f32)
    sig = jax.nn.sigmoid(pre_gate)
    act = pre_gate * sig
    hidden = (act * pre_up).astype(bf16)
    hidden_grad = jnp.dot(row_grad, down_w.T, preferred_element_type=f32)
    up_grad = (hidden_grad * act).astype(bf16)
    gate_grad = (hidden_grad * pre_up * sig * (1.0 + pre_gate * (1.0 - sig))).astype(bf16)
    row_input = jnp.dot(gate_grad, gate_w.T, preferred_element_type=f32)
    row_input = row_input + jnp.dot(up_grad, up_w.T, preferred_element_type=f32)
    back = row_input.astype(bf16).reshape(experts, capacity, width)
    spread = jnp.einsum("ect,ecd->etd", pick, back, preferred_element_type=f32).astype(bf16)
    if experts == 4 * DEPTH:
        grad_input = scatter_sums(spread)
    else:
        grad_input = lax.psum_scatter(
            spread.reshape(experts * tok_rows, width), "expert", scatter_dimension=0, tiled=True
        )
    term_gate = jnp.dot(xrows.T, gate_grad, preferred_element_type=f32).astype(bf16)
    term_up = jnp.dot(xrows.T, up_grad, preferred_element_type=f32).astype(bf16)
    term_down = jnp.dot(hidden.T, row_grad, preferred_element_type=f32).astype(bf16)
    sum_gate = lax.psum_scatter(term_gate, "replica", scatter_dimension=1, tiled=True)
    sum_up = lax.psum_scatter(term_up, "replica", scatter_dimension=1, tiled=True)
    sum_down = lax.psum_scatter(term_down, "replica", scatter_dimension=0, tiled=True)
    return (grad_input, sum_gate[None], sum_up[None], sum_down[None])


def solution(mesh):
    tokens = P(("expert", "replica"), None)
    weights = P("expert", None, None)
    return jax.shard_map(
        shards,
        mesh=mesh,
        in_specs=(tokens,) * 5 + (weights,) * 6,
        out_specs=(
            tokens,
            P("expert", None, "replica"),
            P("expert", None, "replica"),
            P("expert", "replica", None),
        ),
        check_vma=False,
    )
```

```python
import jax
import jax.numpy as jnp
from jax import lax
from jax.experimental import pallas as pl
from jax.experimental.pallas import tpu as pltpu
from jax.sharding import PartitionSpec as P

DEPTH = 4


def place():
    me = lax.axis_index("expert")
    z, q = me // 4, me % 4
    x, y = q % 2, q // 2
    return me, z, q, q + 1 - 2 * x, q + 2 - 4 * y, 3 - q


def greet(me, z, qx, qy):
    barrier = pltpu.get_barrier_semaphore()
    for dev in (4 * z + qx, 4 * z + qy):
        pl.semaphore_signal(barrier, inc=1, device_id={"expert": dev})

    @pl.when(z > 0)
    def _():
        pl.semaphore_signal(barrier, inc=1, device_id={"expert": me - 4})

    @pl.when(z < DEPTH - 1)
    def _():
        pl.semaphore_signal(barrier, inc=1, device_id={"expert": me + 4})

    peers = 2 + jnp.minimum(z, 1) + jnp.minimum(DEPTH - 1 - z, 1)
    pl.semaphore_wait(barrier, peers)


def near_first(zz):
    return sorted(range(DEPTH), key=lambda s: (abs(s - zz), s))


def nt(a, b):
    return lax.dot_general(a, b, (((1,), (1,)), ((), ())), preferred_element_type=jnp.float32)


def rows_kernel(
    x_ref, g_ref, pick, pick_t, gates, gate_w, up_w, down_w,
    part, xrows, row_grad, hidden, gate_grad, up_grad,
    all_x, all_g, part_v, x_v, r_v, h_v, gg_v, ug_v, total,
    send_sem, recv_sem, own_sem, out_sem,
):
    me, z, q, qx, qy, qd = place()
    full, own = (all_x, all_g), (x_ref, g_ref)
    cap, ff, chunk = pick.shape[1], gate_w.shape[1], 256
    rows = 4 * cap
    f32, bf16 = jnp.float32, jnp.bfloat16
    greet(me, z, qx, qy)

    def copy_of(zz, a, block, way):
        mine = block is None
        return pltpu.make_async_remote_copy(
            src_ref=own[a] if mine else full[a].at[block],
            dst_ref=full[a].at[me if mine else block],
            send_sem=send_sem.at[a, me if mine else block, way],
            recv_sem=recv_sem.at[a, me if mine else block],
            device_id={"expert": (4 * zz + qx, 4 * zz + qy, me + 4, me - 4)[way]},
        )

    def arrive(a, block):
        pltpu.make_async_remote_copy(
            src_ref=full[a].at[block],
            dst_ref=full[a].at[block],
            send_sem=send_sem.at[a, block, 0],
            recv_sem=recv_sem.at[a, block],
            device_id={"expert": 4 * z + qx},
        ).wait_recv()

    def column_ways(zz, src):
        ways = []
        if src <= zz < DEPTH - 1:
            ways.append(2)
        if src >= zz > 0:
            ways.append(3)
        return ways + [0, 1]

    def column(zz, src):
        for a in range(2):
            if src != zz:
                arrive(a, 4 * src + q)
            for way in column_ways(zz, src):
                copy_of(zz, a, None if src == zz else 4 * src + q, way).start()

    def talk(zz, i):
        order = near_first(zz)
        if i == 0:
            column(zz, zz)
            for a in range(2):
                pltpu.make_async_copy(own[a], full[a].at[me], own_sem.at[a]).start()
        if i + 1 < DEPTH:
            column(zz, order[i + 1])
        if i < DEPTH:
            arrive(1, 4 * order[i] + qx)
            copy_of(zz, 1, 4 * order[i] + qx, 1).start()
            arrive(0, 4 * order[i] + qy)
            copy_of(zz, 0, 4 * order[i] + qy, 0).start()
        if i == 1:
            for a in range(2):
                pltpu.make_async_copy(own[a], full[a].at[me], own_sem.at[a]).wait()
        if i > 0:
            src = order[i - 1]
            arrive(0, 4 * src + qx)
            arrive(1, 4 * src + qy)
            arrive(0, 4 * src + qd)
            arrive(1, 4 * src + qd)

    def finish(zz):
        for src in near_first(zz):
            for a in range(2):
                for way in column_ways(zz, src):
                    copy_of(zz, a, None if src == zz else 4 * src + q, way).wait_send()
            copy_of(zz, 1, 4 * src + qx, 1).wait_send()
            copy_of(zz, 0, 4 * src + qy, 0).wait_send()

    def results(s):
        at = pl.ds(pl.multiple_of(s * rows, rows), rows)
        pairs = [(part_v, part.at[pl.ds(4 * s, 4)]), (x_v, xrows.at[at]), (r_v, row_grad.at[at])]
        pairs += [(h_v, hidden.at[at]), (gg_v, gate_grad.at[at]), (ug_v, up_grad.at[at])]
        return [pltpu.make_async_copy(a, b, out_sem.at[i]) for i, (a, b) in enumerate(pairs)]

    def work(s):
        def compact(p, carry):
            at = pl.ds(pl.multiple_of(p * cap, cap), cap)
            block = 4 * s + p
            x = jnp.dot(pick[block], all_x[block], preferred_element_type=f32)
            x_v[at, :] = x.astype(bf16)
            r = jnp.dot(pick[block], all_g[block], preferred_element_type=f32)
            r_v[at, :] = (r * gates[block]).astype(bf16)
            return carry

        lax.fori_loop(0, 4, compact, 0)
        total[...] = jnp.zeros_like(total)

        def unit(c, carry):
            at = pl.ds(pl.multiple_of(c * chunk, chunk), chunk)
            wg, wu = gate_w[:, at], up_w[:, at]
            pre_gate = jnp.dot(x_v[...], wg, preferred_element_type=f32)
            pre_up = jnp.dot(x_v[...], wu, preferred_element_type=f32)
            hidden_grad = nt(r_v[...], down_w[at, :])
            sig = 1.0 / (1.0 + jnp.exp(-pre_gate))
            act = pre_gate * sig
            h_v[:, at] = (act * pre_up).astype(bf16)
            ug = (hidden_grad * act).astype(bf16)
            gg = (hidden_grad * pre_up * sig * (1.0 + pre_gate * (1.0 - sig))).astype(bf16)
            ug_v[:, at] = ug
            gg_v[:, at] = gg
            total[...] += nt(gg, wg) + nt(ug, wu)
            return carry

        lax.fori_loop(0, ff // chunk, unit, 0)

        def spread(p, carry):
            at = pl.ds(pl.multiple_of(p * cap, cap), cap)
            back = total[at, :].astype(bf16)
            out = jnp.dot(pick_t[4 * s + p], back, preferred_element_type=f32)
            part_v[p] = out.astype(bf16)
            return carry

        lax.fori_loop(0, 4, spread, 0)

    def step(i, carry):
        s = jnp.int32(0)
        for zz in range(DEPTH):
            for j in range(DEPTH + 1):
                here = (z == zz) & (i == j)
                pl.when(here)(lambda zz=zz, j=j: talk(zz, j))
                if j > 0:
                    s = jnp.where(here, near_first(zz)[j - 1], s)

        @pl.when(i > 1)
        def _():
            for copy in results(0):
                copy.wait()

        @pl.when(i > 0)
        def _():
            work(s)
            for copy in results(s):
                copy.start()

        return carry

    lax.fori_loop(0, DEPTH + 1, step, 0)
    for copy in results(0):
        copy.wait()
    for zz in range(DEPTH):
        pl.when(z == zz)(lambda zz=zz: finish(zz))


def routed_rows(inputs, out_grad, pick, pick_t, gates, gate_w, up_w, down_w):
    tokens, width = inputs.shape
    blocks, cap, _ = pick.shape
    ff = gate_w.shape[1]
    dtype = inputs.dtype
    hbm, vmem = pl.BlockSpec(memory_space=pl.ANY), pl.BlockSpec(memory_space=pltpu.VMEM)
    out = [(blocks, tokens, width)] + [(blocks * cap, width)] * 2 + [(blocks * cap, ff)] * 3
    held = [(blocks, tokens, width)] * 2 + [(4, tokens, width)]
    held += [(4 * cap, width)] * 2 + [(4 * cap, ff)] * 3
    return pl.pallas_call(
        rows_kernel,
        out_shape=tuple(jax.ShapeDtypeStruct(shape, dtype) for shape in out),
        in_specs=[vmem] * 8,
        out_specs=(hbm,) * 6,
        scratch_shapes=[pltpu.VMEM(shape, dtype) for shape in held]
        + [
            pltpu.VMEM((4 * cap, width), jnp.float32),
            pltpu.SemaphoreType.DMA((2, 4 * DEPTH, 4)),
            pltpu.SemaphoreType.DMA((2, 4 * DEPTH)),
            pltpu.SemaphoreType.DMA((2,)),
            pltpu.SemaphoreType.DMA((6,)),
        ],
        compiler_params=pltpu.CompilerParams(
            collective_id=0, has_side_effects=True, vmem_limit_bytes=56 * 1024 * 1024
        ),
    )(inputs, out_grad, pick, pick_t, gates, gate_w, up_w, down_w)


def scatter_kernel(
    part, out, halves, far, near, column, above, send_sem, far_sem, near_sem, above_sem
):
    me, z, q, qx, qy, qd = place()
    rows, width = out.shape
    half = width // 2
    cut = (pl.ds(0, half), pl.ds(half, half))
    step = 16
    greet(me, z, qx, qy)

    def total(dst, terms):
        def body(i, carry):
            at = pl.ds(pl.multiple_of(i * step, step), step)
            acc = terms[0][at, :].astype(jnp.float32)
            for term in terms[1:]:
                acc = acc + term[at, :].astype(jnp.float32)
            dst[at, :] = acc.astype(dst.dtype)
            return carry

        lax.fori_loop(0, rows // step, body, 0)

    def at_depth(zz):
        sent = []
        plane = (4 * zz + qx, 4 * zz + qy)

        def send(src_ref, dst_ref, sem, recv, dev):
            copy = pltpu.make_async_remote_copy(
                src_ref=src_ref,
                dst_ref=dst_ref,
                send_sem=sem,
                recv_sem=recv,
                device_id={"expert": dev},
            )
            copy.start()
            sent.append(copy)

        def arrive(ref, recv):
            pltpu.make_async_remote_copy(
                src_ref=ref,
                dst_ref=ref,
                send_sem=send_sem.at[0, 0],
                recv_sem=recv,
                device_id={"expert": plane[0]},
            ).wait_recv()

        def first(s):
            for h in (0, 1):
                send(
                    part.at[4 * s + qd, :, cut[h]],
                    far.at[h, s],
                    send_sem.at[s, h],
                    far_sem.at[h, s],
                    plane[1 - h],
                )
            for way, block in ((0, 4 * s + qx), (1, 4 * s + qy)):
                h = 1 - way
                send(
                    part.at[block, :, cut[h]],
                    near.at[way, h, s],
                    send_sem.at[s, 2 + way],
                    near_sem.at[way, h, s],
                    plane[way],
                )

        def second(s):
            for way, block in ((0, 4 * s + qx), (1, 4 * s + qy)):
                h = way
                arrive(far.at[h, s], far_sem.at[h, s])
                total(halves.at[way, s], [part.at[block, :, cut[h]], far.at[h, s]])
                send(
                    halves.at[way, s],
                    near.at[way, h, s],
                    send_sem.at[s, 4 + way],
                    near_sem.at[way, h, s],
                    plane[way],
                )

        def third(s):
            slots = []
            if s <= zz < DEPTH - 1:
                slots.append(s)
            if s >= zz > 0:
                slots.append(DEPTH if s == zz else s)
            for way in (0, 1):
                for h in (0, 1):
                    arrive(near.at[way, h, s], near_sem.at[way, h, s])
            for slot in slots:
                arrive(above.at[slot], above_sem.at[slot])
            dst = out if s == zz else column.at[s]
            for h in (0, 1):
                terms = [part.at[4 * s + q, :, cut[h]], near.at[0, h, s], near.at[1, h, s]]
                terms += [above.at[slot, :, cut[h]] for slot in slots]
                total(dst.at[:, cut[h]], terms)
            if s != zz:
                nxt = zz - 1 if s < zz else zz + 1
                slot = DEPTH if s > zz and nxt == s else s
                send(
                    column.at[s],
                    above.at[slot],
                    send_sem.at[s, 6],
                    above_sem.at[slot],
                    me - 4 if s < zz else me + 4,
                )

        order = sorted(range(DEPTH), key=lambda s: (-abs(s - zz), s))
        for i in range(DEPTH + 2):
            if i < DEPTH:
                first(order[i])
            if 0 <= i - 1 < DEPTH:
                second(order[i - 1])
            if 0 <= i - 2 < DEPTH:
                third(order[i - 2])
        for copy in sent:
            copy.wait_send()

    for zz in range(DEPTH):
        pl.when(z == zz)(lambda zz=zz: at_depth(zz))


def scatter_sums(part):
    blocks, rows, width = part.shape
    half = width // 2
    dtype = part.dtype
    return pl.pallas_call(
        scatter_kernel,
        out_shape=jax.ShapeDtypeStruct((rows, width), dtype),
        in_specs=[pl.BlockSpec(memory_space=pltpu.VMEM)],
        out_specs=pl.BlockSpec(memory_space=pltpu.VMEM),
        scratch_shapes=[
            pltpu.VMEM((2, DEPTH, rows, half), dtype),
            pltpu.VMEM((2, DEPTH, rows, half), dtype),
            pltpu.VMEM((2, 2, DEPTH, rows, half), dtype),
            pltpu.VMEM((DEPTH, rows, width), dtype),
            pltpu.VMEM((DEPTH + 1, rows, width), dtype),
            pltpu.SemaphoreType.DMA((DEPTH, 7)),
            pltpu.SemaphoreType.DMA((2, DEPTH)),
            pltpu.SemaphoreType.DMA((2, 2, DEPTH)),
            pltpu.SemaphoreType.DMA((DEPTH + 1,)),
        ],
        compiler_params=pltpu.CompilerParams(
            collective_id=1, has_side_effects=True, vmem_limit_bytes=40 * 1024 * 1024
        ),
    )(part)


def dequant(weight, scale):
    rows, cols = weight.shape
    srows, scols = scale.shape
    blocks = weight.reshape(srows, rows // srows, scols, cols // scols).astype(jnp.float32)
    return (blocks * scale[:, None, :, None]).reshape(rows, cols).astype(jnp.bfloat16)


def shards(
    x_quant, x_scale, out_grad, expert_ids, gate_fixed, w_gate, s_gate, w_up, s_up, w_down, s_down
):
    f32, bf16 = jnp.float32, jnp.bfloat16
    tok_rows, width = x_quant.shape
    topk = expert_ids.shape[1]
    experts = lax.axis_size("expert")
    capacity = tok_rows * topk * 5 // (4 * experts)
    blk_width = width // x_scale.shape[1]
    scaled = x_quant.reshape(tok_rows, -1, blk_width).astype(f32) * x_scale[:, :, None]
    inputs = scaled.reshape(tok_rows, width).astype(bf16)
    named = expert_ids[None, :, :] == jnp.arange(experts, dtype=jnp.int32)[:, None, None]
    units = jnp.sum(jnp.where(named, gate_fixed[None], 0), axis=2).astype(f32)
    units = lax.all_to_all(units, "expert", split_axis=0, concat_axis=0, tiled=True)

    chosen = units > 0
    rank = jnp.cumsum(chosen.astype(jnp.int32), axis=1) - 1
    pick = chosen[:, None, :] & (
        rank[:, None, :] == jnp.arange(capacity, dtype=jnp.int32)[None, :, None]
    )
    gates = jnp.sum(jnp.where(pick, units[:, None, :], 0.0), axis=2) / 65536.0
    pick = pick.astype(bf16)

    gate_w = dequant(w_gate[0], s_gate[0])
    up_w = dequant(w_up[0], s_up[0])
    down_w = dequant(w_down[0], s_down[0])
    rows = experts * capacity
    if experts == 4 * DEPTH:
        spread, xrows, row_grad, hidden, gate_grad, up_grad = routed_rows(
            inputs, out_grad, pick, pick.swapaxes(1, 2), gates[:, :, None], gate_w, up_w, down_w
        )
        grad_input = scatter_sums(spread)
    else:
        all_x = lax.all_gather(inputs, "expert", axis=0, tiled=False)
        all_g = lax.all_gather(out_grad, "expert", axis=0, tiled=False)
        xrows = jnp.einsum("ect,etd->ecd", pick, all_x, preferred_element_type=f32)
        xrows = xrows.astype(bf16).reshape(rows, width)
        row_grad = jnp.einsum("ect,etd->ecd", pick, all_g, preferred_element_type=f32)
        row_grad = (row_grad * gates[:, :, None]).astype(bf16).reshape(rows, width)
        pre_gate = jnp.dot(xrows, gate_w, preferred_element_type=f32)
        pre_up = jnp.dot(xrows, up_w, preferred_element_type=f32)
        sig = jax.nn.sigmoid(pre_gate)
        act = pre_gate * sig
        hidden = (act * pre_up).astype(bf16)
        hidden_grad = jnp.dot(row_grad, down_w.T, preferred_element_type=f32)
        up_grad = (hidden_grad * act).astype(bf16)
        gate_grad = (hidden_grad * pre_up * sig * (1.0 + pre_gate * (1.0 - sig))).astype(bf16)
        row_input = jnp.dot(gate_grad, gate_w.T, preferred_element_type=f32)
        row_input = row_input + jnp.dot(up_grad, up_w.T, preferred_element_type=f32)
        back = row_input.astype(bf16).reshape(experts, capacity, width)
        spread = jnp.einsum("ect,ecd->etd", pick, back, preferred_element_type=f32).astype(bf16)
        grad_input = lax.psum_scatter(
            spread.reshape(experts * tok_rows, width), "expert", scatter_dimension=0, tiled=True
        )
    term_gate = jnp.dot(xrows.T, gate_grad, preferred_element_type=f32).astype(bf16)
    term_up = jnp.dot(xrows.T, up_grad, preferred_element_type=f32).astype(bf16)
    term_down = jnp.dot(hidden.T, row_grad, preferred_element_type=f32).astype(bf16)
    sum_gate = lax.psum_scatter(term_gate, "replica", scatter_dimension=1, tiled=True)
    sum_up = lax.psum_scatter(term_up, "replica", scatter_dimension=1, tiled=True)
    sum_down = lax.psum_scatter(term_down, "replica", scatter_dimension=0, tiled=True)
    return (grad_input, sum_gate[None], sum_up[None], sum_down[None])


def solution(mesh):
    tokens = P(("expert", "replica"), None)
    weights = P("expert", None, None)
    return jax.shard_map(
        shards,
        mesh=mesh,
        in_specs=(tokens,) * 5 + (weights,) * 6,
        out_specs=(
            tokens,
            P("expert", None, "replica"),
            P("expert", None, "replica"),
            P("expert", "replica", None),
        ),
        check_vma=False,
    )
```

```python
import jax
import jax.numpy as jnp
from jax import lax
from jax.experimental import pallas as pl
from jax.experimental.pallas import tpu as pltpu
from jax.sharding import PartitionSpec as P

DEPTH = 4


def place():
    me = lax.axis_index("expert")
    z, q = me // 4, me % 4
    x, y = q % 2, q // 2
    return me, z, q, q + 1 - 2 * x, q + 2 - 4 * y, 3 - q


def greet(me, z, qx, qy, twin=None):
    barrier = pltpu.get_barrier_semaphore()
    if twin is not None:
        pl.semaphore_signal(barrier, inc=1, device_id={"replica": twin})
    for dev in (4 * z + qx, 4 * z + qy):
        pl.semaphore_signal(barrier, inc=1, device_id={"expert": dev})

    @pl.when(z > 0)
    def _():
        pl.semaphore_signal(barrier, inc=1, device_id={"expert": me - 4})

    @pl.when(z < DEPTH - 1)
    def _():
        pl.semaphore_signal(barrier, inc=1, device_id={"expert": me + 4})

    peers = 2 + jnp.minimum(z, 1) + jnp.minimum(DEPTH - 1 - z, 1)
    pl.semaphore_wait(barrier, peers + (twin is not None))


def near_first(zz):
    return sorted(range(DEPTH), key=lambda s: (abs(s - zz), s))


def nt(a, b):
    return lax.dot_general(a, b, (((1,), (1,)), ((), ())), preferred_element_type=jnp.float32)


def rows_kernel(
    x_ref, g_ref, pick, pick_t, gates, gate_q, up_q, down_q, gate_s, up_s, down_s,
    part, xrows, row_grad, hidden, gate_grad, up_grad,
    all_x, all_g, part_v, x_v, r_v, h_v, gg_v, ug_v, total,
    raw_a, raw_b, raw_c, gate_w, up_w, down_w,
    send_sem, recv_sem, own_sem, out_sem, raw_sem,
):
    me, z, q, qx, qy, qd = place()
    full, own = (all_x, all_g), (x_ref, g_ref)
    cap, ff, chunk = pick.shape[1], gate_q.shape[1], 256
    rows = 4 * cap
    f32, bf16 = jnp.float32, jnp.bfloat16
    greet(me, z, qx, qy)

    def copy_of(zz, a, block, way):
        mine = block is None
        return pltpu.make_async_remote_copy(
            src_ref=own[a] if mine else full[a].at[block],
            dst_ref=full[a].at[me if mine else block],
            send_sem=send_sem.at[a, me if mine else block, way],
            recv_sem=recv_sem.at[a, me if mine else block],
            device_id={"expert": (4 * zz + qx, 4 * zz + qy, me + 4, me - 4)[way]},
        )

    def arrive(a, block):
        pltpu.make_async_remote_copy(
            src_ref=full[a].at[block],
            dst_ref=full[a].at[block],
            send_sem=send_sem.at[a, block, 0],
            recv_sem=recv_sem.at[a, block],
            device_id={"expert": 4 * z + qx},
        ).wait_recv()

    def column_ways(zz, src):
        ways = []
        if src <= zz < DEPTH - 1:
            ways.append(2)
        if src >= zz > 0:
            ways.append(3)
        return ways + [0, 1]

    def column(zz, src):
        for a in range(2):
            if src != zz:
                arrive(a, 4 * src + q)
            for way in column_ways(zz, src):
                copy_of(zz, a, None if src == zz else 4 * src + q, way).start()

    def talk(zz, i):
        order = near_first(zz)
        if i + 1 < DEPTH:
            column(zz, order[i + 1])
        if i < DEPTH:
            arrive(1, 4 * order[i] + qx)
            copy_of(zz, 1, 4 * order[i] + qx, 1).start()
            arrive(0, 4 * order[i] + qy)
            copy_of(zz, 0, 4 * order[i] + qy, 0).start()
        if i == 1:
            for a in range(2):
                pltpu.make_async_copy(own[a], full[a].at[me], own_sem.at[a]).wait()
        if i > 0:
            src = order[i - 1]
            arrive(0, 4 * src + qx)
            arrive(1, 4 * src + qy)
            arrive(0, 4 * src + qd)
            arrive(1, 4 * src + qd)

    def finish(zz):
        for src in near_first(zz):
            for a in range(2):
                for way in column_ways(zz, src):
                    copy_of(zz, a, None if src == zz else 4 * src + q, way).wait_send()
            copy_of(zz, 1, 4 * src + qx, 1).wait_send()
            copy_of(zz, 0, 4 * src + qy, 0).wait_send()

    def results(s):
        at = pl.ds(pl.multiple_of(s * rows, rows), rows)
        pairs = [(part_v, part.at[pl.ds(4 * s, 4)]), (x_v, xrows.at[at]), (r_v, row_grad.at[at])]
        pairs += [(h_v, hidden.at[at]), (gg_v, gate_grad.at[at]), (ug_v, up_grad.at[at])]
        return [pltpu.make_async_copy(a, b, out_sem.at[i]) for i, (a, b) in enumerate(pairs)]

    def work(s):
        def compact(p, carry):
            at = pl.ds(pl.multiple_of(p * cap, cap), cap)
            block = 4 * s + p
            x = jnp.dot(pick[block], all_x[block], preferred_element_type=f32)
            x_v[at, :] = x.astype(bf16)
            r = jnp.dot(pick[block], all_g[block], preferred_element_type=f32)
            r_v[at, :] = (r * gates[block]).astype(bf16)
            return carry

        lax.fori_loop(0, 4, compact, 0)
        total[...] = jnp.zeros_like(total)

        def unit(c, carry):
            at = pl.ds(pl.multiple_of(c * chunk, chunk), chunk)
            wg, wu = gate_w[:, at], up_w[:, at]
            pre_gate = jnp.dot(x_v[...], wg, preferred_element_type=f32)
            pre_up = jnp.dot(x_v[...], wu, preferred_element_type=f32)
            hidden_grad = nt(r_v[...], down_w[at, :])
            sig = 1.0 / (1.0 + jnp.exp(-pre_gate))
            act = pre_gate * sig
            h_v[:, at] = (act * pre_up).astype(bf16)
            ug = (hidden_grad * act).astype(bf16)
            gg = (hidden_grad * pre_up * sig * (1.0 + pre_gate * (1.0 - sig))).astype(bf16)
            ug_v[:, at] = ug
            gg_v[:, at] = gg
            total[...] += nt(gg, wg) + nt(ug, wu)
            return carry

        lax.fori_loop(0, ff // chunk, unit, 0)

        def spread(p, carry):
            at = pl.ds(pl.multiple_of(p * cap, cap), cap)
            back = total[at, :].astype(bf16)
            out = jnp.dot(pick_t[4 * s + p], back, preferred_element_type=f32)
            part_v[p] = out.astype(bf16)
            return carry

        lax.fori_loop(0, 4, spread, 0)

    def begin(zz):
        column(zz, zz)
        for a in range(2):
            pltpu.make_async_copy(own[a], full[a].at[me], own_sem.at[a]).start()

    def dequantize(raw, scale, weight):
        def body(i, carry):
            at = pl.ds(pl.multiple_of(i * 128, 128), 128)
            for j in range(weight.shape[1] // 128):
                cols = pl.ds(j * 128, 128)
                weight[at, cols] = (raw[at, cols].astype(f32) * scale[i, j]).astype(bf16)
            return carry

        lax.fori_loop(0, weight.shape[0] // 128, body, 0)

    raws = ((gate_q, raw_a), (up_q, raw_b), (down_q, raw_c))
    loads = [pltpu.make_async_copy(a, b, raw_sem.at[i]) for i, (a, b) in enumerate(raws)]
    for zz in range(DEPTH):
        pl.when(z == zz)(lambda zz=zz: begin(zz))
    for load in loads:
        load.start()
    for load, raw, scale, weight in zip(
        loads, (raw_a, raw_b, raw_c), (gate_s, up_s, down_s), (gate_w, up_w, down_w)
    ):
        load.wait()
        dequantize(raw, scale, weight)

    def step(i, carry):
        s = jnp.int32(0)
        for zz in range(DEPTH):
            for j in range(DEPTH + 1):
                here = (z == zz) & (i == j)
                pl.when(here)(lambda zz=zz, j=j: talk(zz, j))
                if j > 0:
                    s = jnp.where(here, near_first(zz)[j - 1], s)

        @pl.when(i > 1)
        def _():
            for copy in results(0):
                copy.wait()

        @pl.when(i > 0)
        def _():
            work(s)
            for copy in results(s):
                copy.start()

        return carry

    lax.fori_loop(0, DEPTH + 1, step, 0)
    for copy in results(0):
        copy.wait()
    for zz in range(DEPTH):
        pl.when(z == zz)(lambda zz=zz: finish(zz))


def routed_rows(inputs, out_grad, pick, pick_t, gates, weights, scales):
    tokens, width = inputs.shape
    blocks, cap, _ = pick.shape
    ff = weights[0].shape[1]
    dtype = inputs.dtype
    hbm, vmem = pl.BlockSpec(memory_space=pl.ANY), pl.BlockSpec(memory_space=pltpu.VMEM)
    out = [(blocks, tokens, width)] + [(blocks * cap, width)] * 2 + [(blocks * cap, ff)] * 3
    held = [(blocks, tokens, width)] * 2 + [(4, tokens, width)]
    held += [(4 * cap, width)] * 2 + [(4 * cap, ff)] * 3
    return pl.pallas_call(
        rows_kernel,
        out_shape=tuple(jax.ShapeDtypeStruct(shape, dtype) for shape in out),
        in_specs=[vmem] * 5 + [hbm] * 3 + [pl.BlockSpec(memory_space=pltpu.SMEM)] * 3,
        out_specs=(hbm,) * 6,
        scratch_shapes=[pltpu.VMEM(shape, dtype) for shape in held]
        + [
            pltpu.VMEM((4 * cap, width), jnp.float32),
            *[pltpu.VMEM(w.shape, dtype) for w in weights * 2],
            pltpu.SemaphoreType.DMA((2, 4 * DEPTH, 4)),
            pltpu.SemaphoreType.DMA((2, 4 * DEPTH)),
            pltpu.SemaphoreType.DMA((2,)),
            pltpu.SemaphoreType.DMA((6,)),
            pltpu.SemaphoreType.DMA((3,)),
        ],
        compiler_params=pltpu.CompilerParams(
            collective_id=0, has_side_effects=True, vmem_limit_bytes=56 * 1024 * 1024
        ),
    )(inputs, out_grad, pick, pick_t, gates, *weights, *scales)


def scatter_kernel(
    part, xrows, row_grad, hidden, gate_grad, up_grad,
    out, sum_gate, sum_up, sum_down,
    halves, far, near, column, above, give_gate, give_up, give_down, got_gate, got_up, got_down,
    send_sem, far_sem, near_sem, above_sem, give_sem, got_sem,
):
    me, z, q, qx, qy, qd = place()
    core = lax.axis_index("replica")
    rows, width = out.shape
    half = width // 2
    cut = (pl.ds(0, half), pl.ds(half, half))
    step = 16
    f32 = jnp.float32
    greet(me, z, qx, qy, 1 - core)

    def total(dst, terms):
        def body(i, carry):
            at = pl.ds(pl.multiple_of(i * step, step), step)
            acc = terms[0][at, :].astype(f32)
            for term in terms[1:]:
                acc = acc + term[at, :].astype(f32)
            dst[at, :] = acc.astype(dst.dtype)
            return carry

        lax.fori_loop(0, rows // step, body, 0)

    def copy_of(src_ref, dst_ref, sem, recv, dev):
        return pltpu.make_async_remote_copy(
            src_ref=src_ref,
            dst_ref=dst_ref,
            send_sem=sem,
            recv_sem=recv,
            device_id={"expert": dev},
        )

    def arrive(ref, recv):
        copy_of(ref, ref, send_sem.at[0, 0], recv, 4 * z + qx).wait_recv()

    def first(zz, s):
        plane = (4 * zz + qx, 4 * zz + qy)
        copies = []
        for h in (0, 1):
            copies.append(
                copy_of(
                    part.at[4 * s + qd, :, cut[h]],
                    far.at[h, s],
                    send_sem.at[s, h],
                    far_sem.at[h, s],
                    plane[1 - h],
                )
            )
        for way, block in ((0, 4 * s + qx), (1, 4 * s + qy)):
            h = 1 - way
            copies.append(
                copy_of(
                    part.at[block, :, cut[h]],
                    near.at[way, h, s],
                    send_sem.at[s, 2 + way],
                    near_sem.at[way, h, s],
                    plane[way],
                )
            )
        return copies

    def second(zz, s, way):
        return copy_of(
            halves.at[way, s],
            near.at[way, way, s],
            send_sem.at[s, 4 + way],
            near_sem.at[way, way, s],
            4 * zz + (qx, qy)[way],
        )

    def third(zz, s):
        slot = DEPTH if s > zz and zz + 1 == s else s
        return copy_of(
            column.at[s],
            above.at[slot],
            send_sem.at[s, 6],
            above_sem.at[slot],
            me - 4 if s < zz else me + 4,
        )

    def relay(zz, s):
        for way, block in ((0, 4 * s + qx), (1, 4 * s + qy)):
            arrive(far.at[way, s], far_sem.at[way, s])
            total(halves.at[way, s], [part.at[block, :, cut[way]], far.at[way, s]])
            second(zz, s, way).start()

    def add(zz, s):
        slots = []
        if s <= zz < DEPTH - 1:
            slots.append(s)
        if s >= zz > 0:
            slots.append(DEPTH if s == zz else s)
        for way in (0, 1):
            for h in (0, 1):
                arrive(near.at[way, h, s], near_sem.at[way, h, s])
        for slot in slots:
            arrive(above.at[slot], above_sem.at[slot])
        dst = out if s == zz else column.at[s]
        for h in (0, 1):
            terms = [part.at[4 * s + q, :, cut[h]], near.at[0, h, s], near.at[1, h, s]]
            terms += [above.at[slot, :, cut[h]] for slot in slots]
            total(dst.at[:, cut[h]], terms)
        if s != zz:
            third(zz, s).start()

    def talk(zz, i):
        order = near_first(zz)[::-1]
        if i < DEPTH:
            for copy in first(zz, order[i]):
                copy.start()
        if 0 <= i - 1 < DEPTH:
            relay(zz, order[i - 1])
        if 0 <= i - 2 < DEPTH:
            add(zz, order[i - 2])

    def finish(zz):
        for s in range(DEPTH):
            for copy in first(zz, s):
                copy.wait_send()
            for way in (0, 1):
                second(zz, s, way).wait_send()
            if s != zz:
                third(zz, s).wait_send()

    lots = (
        (xrows, gate_grad, give_gate, got_gate, sum_gate),
        (xrows, up_grad, give_up, got_up, sum_up),
        (hidden, row_grad, give_down, got_down, sum_down),
    )

    def give(k):
        return pltpu.make_async_remote_copy(
            src_ref=lots[k][2],
            dst_ref=lots[k][3],
            send_sem=give_sem.at[k],
            recv_sem=got_sem.at[k],
            device_id={"replica": 1 - core},
        )

    def product(k, side, emit):
        left, right = lots[k][:2]
        chunk = 512
        ff = hidden.shape[1] // 2
        units = pl.ds(pl.multiple_of(side * ff, ff), ff)

        def body(c, carry):
            at = pl.ds(pl.multiple_of(c * chunk, chunk), chunk)
            a = left[:, at] if k < 2 else left[:, units]
            b = right[:, units] if k < 2 else right[:, at]
            acc = lax.dot_general(a, b, (((0,), (0,)), ((), ())), preferred_element_type=f32)
            emit((at, slice(None)) if k < 2 else (slice(None), at), acc)
            return carry

        lax.fori_loop(0, width // chunk, body, 0)

    def work(k, last):
        kept, got, dst = lots[k][2:]

        def emit_other(at, acc):
            kept[at] = acc.astype(kept.dtype)

        def emit_own(at, acc):
            dst[at] = (acc + got[at].astype(f32)).astype(dst.dtype)

        if last:
            give(k).wait_recv()
            product(k, core, emit_own)
        else:
            product(k, 1 - core, emit_other)
            give(k).start()

    def turn(i, carry):
        for j in range(DEPTH + 2):
            for zz in range(DEPTH):
                pl.when((z == zz) & (i == j))(lambda zz=zz, j=j: talk(zz, j))
            pl.when(i == j)(lambda j=j: work(j % 3, j >= 3))
        return carry

    lax.fori_loop(0, DEPTH + 2, turn, 0)
    for k in range(3):
        give(k).wait_send()
    for zz in range(DEPTH):
        pl.when(z == zz)(lambda zz=zz: finish(zz))


def scatter_sums(part, xrows, row_grad, hidden, gate_grad, up_grad):
    blocks, rows, width = part.shape
    half, ff = width // 2, hidden.shape[1] // 2
    dtype = part.dtype
    vmem = pl.BlockSpec(memory_space=pltpu.VMEM)
    lots = [(width, ff), (width, ff), (ff, width)]
    held = [
        (2, DEPTH, rows, half),
        (2, DEPTH, rows, half),
        (2, 2, DEPTH, rows, half),
        (DEPTH, rows, width),
        (DEPTH + 1, rows, width),
    ]
    return pl.pallas_call(
        scatter_kernel,
        out_shape=tuple(jax.ShapeDtypeStruct(shape, dtype) for shape in [(rows, width), *lots]),
        in_specs=[vmem] * 6,
        out_specs=(vmem,) * 4,
        scratch_shapes=[pltpu.VMEM(shape, dtype) for shape in held + lots + lots]
        + [
            pltpu.SemaphoreType.DMA((DEPTH, 7)),
            pltpu.SemaphoreType.DMA((2, DEPTH)),
            pltpu.SemaphoreType.DMA((2, 2, DEPTH)),
            pltpu.SemaphoreType.DMA((DEPTH + 1,)),
            pltpu.SemaphoreType.DMA((3,)),
            pltpu.SemaphoreType.DMA((3,)),
        ],
        compiler_params=pltpu.CompilerParams(
            collective_id=1, has_side_effects=True, vmem_limit_bytes=58 * 1024 * 1024
        ),
    )(part, xrows, row_grad, hidden, gate_grad, up_grad)


def dequant(weight, scale):
    rows, cols = weight.shape
    srows, scols = scale.shape
    blocks = weight.reshape(srows, rows // srows, scols, cols // scols).astype(jnp.float32)
    return (blocks * scale[:, None, :, None]).reshape(rows, cols).astype(jnp.bfloat16)


def shards(
    x_quant, x_scale, out_grad, expert_ids, gate_fixed, w_gate, s_gate, w_up, s_up, w_down, s_down
):
    f32, bf16 = jnp.float32, jnp.bfloat16
    tok_rows, width = x_quant.shape
    topk = expert_ids.shape[1]
    experts = lax.axis_size("expert")
    capacity = tok_rows * topk * 5 // (4 * experts)
    blk_width = width // x_scale.shape[1]
    scaled = x_quant.reshape(tok_rows, -1, blk_width).astype(f32) * x_scale[:, :, None]
    inputs = scaled.reshape(tok_rows, width).astype(bf16)
    named = expert_ids[None, :, :] == jnp.arange(experts, dtype=jnp.int32)[:, None, None]
    units = jnp.sum(jnp.where(named, gate_fixed[None], 0), axis=2).astype(f32)
    units = lax.all_to_all(units, "expert", split_axis=0, concat_axis=0, tiled=True)

    chosen = units > 0
    rank = jnp.cumsum(chosen.astype(jnp.int32), axis=1) - 1
    pick = chosen[:, None, :] & (
        rank[:, None, :] == jnp.arange(capacity, dtype=jnp.int32)[None, :, None]
    )
    gates = jnp.sum(jnp.where(pick, units[:, None, :], 0.0), axis=2) / 65536.0
    pick = pick.astype(bf16)

    if experts == 4 * DEPTH:
        moved = routed_rows(
            inputs,
            out_grad,
            pick,
            pick.swapaxes(1, 2),
            gates[:, :, None],
            [w_gate[0], w_up[0], w_down[0]],
            [s_gate[0], s_up[0], s_down[0]],
        )
        grad_input, sum_gate, sum_up, sum_down = scatter_sums(*moved)
        return (grad_input, sum_gate[None], sum_up[None], sum_down[None])

    gate_w = dequant(w_gate[0], s_gate[0])
    up_w = dequant(w_up[0], s_up[0])
    down_w = dequant(w_down[0], s_down[0])
    rows = experts * capacity
    all_x = lax.all_gather(inputs, "expert", axis=0, tiled=False)
    all_g = lax.all_gather(out_grad, "expert", axis=0, tiled=False)
    xrows = jnp.einsum("ect,etd->ecd", pick, all_x, preferred_element_type=f32)
    xrows = xrows.astype(bf16).reshape(rows, width)
    row_grad = jnp.einsum("ect,etd->ecd", pick, all_g, preferred_element_type=f32)
    row_grad = (row_grad * gates[:, :, None]).astype(bf16).reshape(rows, width)
    pre_gate = jnp.dot(xrows, gate_w, preferred_element_type=f32)
    pre_up = jnp.dot(xrows, up_w, preferred_element_type=f32)
    sig = jax.nn.sigmoid(pre_gate)
    act = pre_gate * sig
    hidden = (act * pre_up).astype(bf16)
    hidden_grad = jnp.dot(row_grad, down_w.T, preferred_element_type=f32)
    up_grad = (hidden_grad * act).astype(bf16)
    gate_grad = (hidden_grad * pre_up * sig * (1.0 + pre_gate * (1.0 - sig))).astype(bf16)
    row_input = jnp.dot(gate_grad, gate_w.T, preferred_element_type=f32)
    row_input = row_input + jnp.dot(up_grad, up_w.T, preferred_element_type=f32)
    back = row_input.astype(bf16).reshape(experts, capacity, width)
    spread = jnp.einsum("ect,ecd->etd", pick, back, preferred_element_type=f32).astype(bf16)
    grad_input = lax.psum_scatter(
        spread.reshape(experts * tok_rows, width), "expert", scatter_dimension=0, tiled=True
    )
    term_gate = jnp.dot(xrows.T, gate_grad, preferred_element_type=f32).astype(bf16)
    term_up = jnp.dot(xrows.T, up_grad, preferred_element_type=f32).astype(bf16)
    term_down = jnp.dot(hidden.T, row_grad, preferred_element_type=f32).astype(bf16)
    sum_gate = lax.psum_scatter(term_gate, "replica", scatter_dimension=1, tiled=True)
    sum_up = lax.psum_scatter(term_up, "replica", scatter_dimension=1, tiled=True)
    sum_down = lax.psum_scatter(term_down, "replica", scatter_dimension=0, tiled=True)
    return (grad_input, sum_gate[None], sum_up[None], sum_down[None])


def solution(mesh):
    tokens = P(("expert", "replica"), None)
    weights = P("expert", None, None)
    return jax.shard_map(
        shards,
        mesh=mesh,
        in_specs=(tokens,) * 5 + (weights,) * 6,
        out_specs=(
            tokens,
            P("expert", None, "replica"),
            P("expert", None, "replica"),
            P("expert", "replica", None),
        ),
        check_vma=False,
    )
```

```python
import jax
import jax.numpy as jnp
from jax import lax
from jax.experimental import pallas as pl
from jax.experimental.pallas import tpu as pltpu
from jax.sharding import PartitionSpec as P

DEPTH = 4


def place():
    me = lax.axis_index("expert")
    z, q = me // 4, me % 4
    x, y = q % 2, q // 2
    return me, z, q, q + 1 - 2 * x, q + 2 - 4 * y, 3 - q


def greet(me, z, qx, qy, twin=None):
    barrier = pltpu.get_barrier_semaphore()
    if twin is not None:
        pl.semaphore_signal(barrier, inc=1, device_id={"replica": twin})
    for dev in (4 * z + qx, 4 * z + qy):
        pl.semaphore_signal(barrier, inc=1, device_id={"expert": dev})

    @pl.when(z > 0)
    def _():
        pl.semaphore_signal(barrier, inc=1, device_id={"expert": me - 4})

    @pl.when(z < DEPTH - 1)
    def _():
        pl.semaphore_signal(barrier, inc=1, device_id={"expert": me + 4})

    peers = 2 + jnp.minimum(z, 1) + jnp.minimum(DEPTH - 1 - z, 1)
    pl.semaphore_wait(barrier, peers + (twin is not None))


def near_first(zz):
    return sorted(range(DEPTH), key=lambda s: (abs(s - zz), s))


def nt(a, b):
    return lax.dot_general(a, b, (((1,), (1,)), ((), ())), preferred_element_type=jnp.float32)


def rows_kernel(
    x_ref, g_ref, pick, pick_t, gates, gate_q, up_q, down_q, gate_s, up_s, down_s,
    part, xrows, row_grad, hidden, gate_grad, up_grad,
    all_x, all_g, part_v, x_v, r_v, h_v, gg_v, ug_v, total,
    raw_a, raw_b, raw_c, gate_w, up_w, down_w,
    send_sem, recv_sem, own_sem, out_sem, raw_sem,
):
    me, z, q, qx, qy, qd = place()
    full, own = (all_x, all_g), (x_ref, g_ref)
    cap, ff, chunk = pick.shape[1], gate_q.shape[1], 256
    rows = 4 * cap
    f32, bf16 = jnp.float32, jnp.bfloat16
    greet(me, z, qx, qy)

    def copy_of(zz, a, block, way):
        mine = block is None
        return pltpu.make_async_remote_copy(
            src_ref=own[a] if mine else full[a].at[block],
            dst_ref=full[a].at[me if mine else block],
            send_sem=send_sem.at[a, me if mine else block, way],
            recv_sem=recv_sem.at[a, me if mine else block],
            device_id={"expert": (4 * zz + qx, 4 * zz + qy, me + 4, me - 4)[way]},
        )

    def arrive(a, block):
        pltpu.make_async_remote_copy(
            src_ref=full[a].at[block],
            dst_ref=full[a].at[block],
            send_sem=send_sem.at[a, block, 0],
            recv_sem=recv_sem.at[a, block],
            device_id={"expert": 4 * z + qx},
        ).wait_recv()

    def column_ways(zz, src):
        ways = []
        if src <= zz < DEPTH - 1:
            ways.append(2)
        if src >= zz > 0:
            ways.append(3)
        return ways + [0, 1]

    def column(zz, src):
        for a in range(2):
            if src != zz:
                arrive(a, 4 * src + q)
            for way in column_ways(zz, src):
                copy_of(zz, a, None if src == zz else 4 * src + q, way).start()

    def talk(zz, i):
        order = near_first(zz)
        if i + 1 < DEPTH:
            column(zz, order[i + 1])
        if i < DEPTH:
            arrive(1, 4 * order[i] + qx)
            copy_of(zz, 1, 4 * order[i] + qx, 1).start()
            arrive(0, 4 * order[i] + qy)
            copy_of(zz, 0, 4 * order[i] + qy, 0).start()
        if i == 1:
            for a in range(2):
                pltpu.make_async_copy(own[a], full[a].at[me], own_sem.at[a]).wait()
        if i > 0:
            src = order[i - 1]
            arrive(0, 4 * src + qx)
            arrive(1, 4 * src + qy)
            arrive(0, 4 * src + qd)
            arrive(1, 4 * src + qd)

    def finish(zz):
        for src in near_first(zz):
            for a in range(2):
                for way in column_ways(zz, src):
                    copy_of(zz, a, None if src == zz else 4 * src + q, way).wait_send()
            copy_of(zz, 1, 4 * src + qx, 1).wait_send()
            copy_of(zz, 0, 4 * src + qy, 0).wait_send()

    def results(s):
        at = pl.ds(pl.multiple_of(s * rows, rows), rows)
        pairs = [(part_v, part.at[pl.ds(4 * s, 4)]), (x_v, xrows.at[at]), (r_v, row_grad.at[at])]
        pairs += [(h_v, hidden.at[at]), (gg_v, gate_grad.at[at]), (ug_v, up_grad.at[at])]
        return [pltpu.make_async_copy(a, b, out_sem.at[i]) for i, (a, b) in enumerate(pairs)]

    def work(s):
        def compact(p, carry):
            at = pl.ds(pl.multiple_of(p * cap, cap), cap)
            block = 4 * s + p
            x = jnp.dot(pick[block], all_x[block], preferred_element_type=f32)
            x_v[at, :] = x.astype(bf16)
            r = jnp.dot(pick[block], all_g[block], preferred_element_type=f32)
            r_v[at, :] = (r * gates[block]).astype(bf16)
            return carry

        lax.fori_loop(0, 4, compact, 0)
        total[...] = jnp.zeros_like(total)

        def unit(c, carry):
            at = pl.ds(pl.multiple_of(c * chunk, chunk), chunk)
            wg, wu = gate_w[:, at], up_w[:, at]
            pre_gate = jnp.dot(x_v[...], wg, preferred_element_type=f32)
            pre_up = jnp.dot(x_v[...], wu, preferred_element_type=f32)
            hidden_grad = nt(r_v[...], down_w[at, :])
            sig = 1.0 / (1.0 + jnp.exp(-pre_gate))
            act = pre_gate * sig
            h_v[:, at] = (act * pre_up).astype(bf16)
            ug = (hidden_grad * act).astype(bf16)
            gg = (hidden_grad * pre_up * sig * (1.0 + pre_gate * (1.0 - sig))).astype(bf16)
            ug_v[:, at] = ug
            gg_v[:, at] = gg
            total[...] += nt(gg, wg) + nt(ug, wu)
            return carry

        lax.fori_loop(0, ff // chunk, unit, 0)

        def spread(p, carry):
            at = pl.ds(pl.multiple_of(p * cap, cap), cap)
            back = total[at, :].astype(bf16)
            out = jnp.dot(pick_t[4 * s + p], back, preferred_element_type=f32)
            part_v[p] = out.astype(bf16)
            return carry

        lax.fori_loop(0, 4, spread, 0)

    def begin(zz):
        column(zz, zz)
        for a in range(2):
            pltpu.make_async_copy(own[a], full[a].at[me], own_sem.at[a]).start()

    def dequantize(raw, scale, weight):
        def body(i, carry):
            at = pl.ds(pl.multiple_of(i * 128, 128), 128)
            for j in range(weight.shape[1] // 128):
                cols = pl.ds(j * 128, 128)
                weight[at, cols] = (raw[at, cols].astype(f32) * scale[i, j]).astype(bf16)
            return carry

        lax.fori_loop(0, weight.shape[0] // 128, body, 0)

    raws = ((gate_q, raw_a), (up_q, raw_b), (down_q, raw_c))
    loads = [pltpu.make_async_copy(a, b, raw_sem.at[i]) for i, (a, b) in enumerate(raws)]
    for zz in range(DEPTH):
        pl.when(z == zz)(lambda zz=zz: begin(zz))
    for load in loads:
        load.start()
    for load, raw, scale, weight in zip(
        loads, (raw_a, raw_b, raw_c), (gate_s, up_s, down_s), (gate_w, up_w, down_w)
    ):
        load.wait()
        dequantize(raw, scale, weight)

    def step(i, carry):
        s = jnp.int32(0)
        for zz in range(DEPTH):
            for j in range(DEPTH + 1):
                here = (z == zz) & (i == j)
                pl.when(here)(lambda zz=zz, j=j: talk(zz, j))
                if j > 0:
                    s = jnp.where(here, near_first(zz)[j - 1], s)

        @pl.when(i > 1)
        def _():
            for copy in results(0):
                copy.wait()

        @pl.when(i > 0)
        def _():
            work(s)
            for copy in results(s):
                copy.start()

        return carry

    lax.fori_loop(0, DEPTH + 1, step, 0)
    for copy in results(0):
        copy.wait()
    for zz in range(DEPTH):
        pl.when(z == zz)(lambda zz=zz: finish(zz))


def routed_rows(inputs, out_grad, pick, pick_t, gates, weights, scales):
    tokens, width = inputs.shape
    blocks, cap, _ = pick.shape
    ff = weights[0].shape[1]
    dtype = inputs.dtype
    hbm, vmem = pl.BlockSpec(memory_space=pl.ANY), pl.BlockSpec(memory_space=pltpu.VMEM)
    out = [(blocks, tokens, width)] + [(blocks * cap, width)] * 2 + [(blocks * cap, ff)] * 3
    held = [(blocks, tokens, width)] * 2 + [(4, tokens, width)]
    held += [(4 * cap, width)] * 2 + [(4 * cap, ff)] * 3
    return pl.pallas_call(
        rows_kernel,
        out_shape=tuple(jax.ShapeDtypeStruct(shape, dtype) for shape in out),
        in_specs=[vmem] * 5 + [hbm] * 3 + [pl.BlockSpec(memory_space=pltpu.SMEM)] * 3,
        out_specs=(hbm,) * 6,
        scratch_shapes=[pltpu.VMEM(shape, dtype) for shape in held]
        + [
            pltpu.VMEM((4 * cap, width), jnp.float32),
            *[pltpu.VMEM(w.shape, dtype) for w in weights * 2],
            pltpu.SemaphoreType.DMA((2, 4 * DEPTH, 4)),
            pltpu.SemaphoreType.DMA((2, 4 * DEPTH)),
            pltpu.SemaphoreType.DMA((2,)),
            pltpu.SemaphoreType.DMA((6,)),
            pltpu.SemaphoreType.DMA((3,)),
        ],
        compiler_params=pltpu.CompilerParams(
            collective_id=0, has_side_effects=True, vmem_limit_bytes=56 * 1024 * 1024
        ),
    )(inputs, out_grad, pick, pick_t, gates, *weights, *scales)


def scatter_kernel(
    part, xrows, row_grad, hidden, gate_grad, up_grad,
    out, sum_gate, sum_up, sum_down,
    halves, far, near, column, above, give_gate, give_up, give_down, got_gate, got_up, got_down,
    send_sem, far_sem, near_sem, above_sem, give_sem, got_sem,
):
    me, z, q, qx, qy, qd = place()
    core = lax.axis_index("replica")
    rows, width = out.shape
    half = width // 2
    cut = (pl.ds(0, half), pl.ds(half, half))
    step = 16
    f32 = jnp.float32
    greet(me, z, qx, qy, 1 - core)

    def total(dst, terms):
        def body(i, carry):
            at = pl.ds(pl.multiple_of(i * step, step), step)
            acc = terms[0][at, :].astype(f32)
            for term in terms[1:]:
                acc = acc + term[at, :].astype(f32)
            dst[at, :] = acc.astype(dst.dtype)
            return carry

        lax.fori_loop(0, rows // step, body, 0)

    def copy_of(src_ref, dst_ref, sem, recv, dev):
        return pltpu.make_async_remote_copy(
            src_ref=src_ref,
            dst_ref=dst_ref,
            send_sem=sem,
            recv_sem=recv,
            device_id={"expert": dev},
        )

    def arrive(ref, recv):
        copy_of(ref, ref, send_sem.at[0, 0], recv, 4 * z + qx).wait_recv()

    def first(zz, s):
        plane = (4 * zz + qx, 4 * zz + qy)
        copies = []
        for h in (0, 1):
            copies.append(
                copy_of(
                    part.at[4 * s + qd, :, cut[h]],
                    far.at[h, s],
                    send_sem.at[s, h],
                    far_sem.at[h, s],
                    plane[1 - h],
                )
            )
        for way, block in ((0, 4 * s + qx), (1, 4 * s + qy)):
            h = 1 - way
            copies.append(
                copy_of(
                    part.at[block, :, cut[h]],
                    near.at[way, h, s],
                    send_sem.at[s, 2 + way],
                    near_sem.at[way, h, s],
                    plane[way],
                )
            )
        return copies

    def second(zz, s, way):
        return copy_of(
            halves.at[way, s],
            near.at[way, way, s],
            send_sem.at[s, 4 + way],
            near_sem.at[way, way, s],
            4 * zz + (qx, qy)[way],
        )

    def third(zz, s):
        slot = DEPTH if s > zz and zz + 1 == s else s
        return copy_of(
            column.at[s],
            above.at[slot],
            send_sem.at[s, 6],
            above_sem.at[slot],
            me - 4 if s < zz else me + 4,
        )

    def relay(zz, s):
        for way, block in ((0, 4 * s + qx), (1, 4 * s + qy)):
            arrive(far.at[way, s], far_sem.at[way, s])
            total(halves.at[way, s], [part.at[block, :, cut[way]], far.at[way, s]])
            second(zz, s, way).start()

    def add(zz, s):
        slots = []
        if s <= zz < DEPTH - 1:
            slots.append(s)
        if s >= zz > 0:
            slots.append(DEPTH if s == zz else s)
        for way in (0, 1):
            for h in (0, 1):
                arrive(near.at[way, h, s], near_sem.at[way, h, s])
        for slot in slots:
            arrive(above.at[slot], above_sem.at[slot])
        dst = out if s == zz else column.at[s]
        for h in (0, 1):
            terms = [part.at[4 * s + q, :, cut[h]], near.at[0, h, s], near.at[1, h, s]]
            terms += [above.at[slot, :, cut[h]] for slot in slots]
            total(dst.at[:, cut[h]], terms)
        if s != zz:
            third(zz, s).start()

    def talk(zz, i):
        order = near_first(zz)[::-1]
        for s in order[:2] if i == 0 else order[i + 1 : i + 2]:
            for copy in first(zz, s):
                copy.start()
        if 0 <= i - 1 < DEPTH:
            relay(zz, order[i - 1])
        if 0 <= i - 2 < DEPTH:
            add(zz, order[i - 2])

    def finish(zz):
        for s in range(DEPTH):
            for copy in first(zz, s):
                copy.wait_send()
            for way in (0, 1):
                second(zz, s, way).wait_send()
            if s != zz:
                third(zz, s).wait_send()

    lots = (
        (xrows, gate_grad, give_gate, got_gate, sum_gate),
        (xrows, up_grad, give_up, got_up, sum_up),
        (hidden, row_grad, give_down, got_down, sum_down),
    )

    def give(k):
        return pltpu.make_async_remote_copy(
            src_ref=lots[k][2],
            dst_ref=lots[k][3],
            send_sem=give_sem.at[k],
            recv_sem=got_sem.at[k],
            device_id={"replica": 1 - core},
        )

    def product(k, side, emit):
        left, right = lots[k][:2]
        chunk = 512
        ff = hidden.shape[1] // 2
        units = pl.ds(pl.multiple_of(side * ff, ff), ff)

        def body(c, carry):
            at = pl.ds(pl.multiple_of(c * chunk, chunk), chunk)
            a = left[:, at] if k < 2 else left[:, units]
            b = right[:, units] if k < 2 else right[:, at]
            acc = lax.dot_general(a, b, (((0,), (0,)), ((), ())), preferred_element_type=f32)
            emit((at, slice(None)) if k < 2 else (slice(None), at), acc)
            return carry

        lax.fori_loop(0, width // chunk, body, 0)

    def work(k, last):
        kept, got, dst = lots[k][2:]

        def emit_other(at, acc):
            kept[at] = acc.astype(kept.dtype)

        def emit_own(at, acc):
            dst[at] = (acc + got[at].astype(f32)).astype(dst.dtype)

        if last:
            give(k).wait_recv()
            product(k, core, emit_own)
        else:
            product(k, 1 - core, emit_other)
            give(k).start()

    def turn(i, carry):
        for j in range(DEPTH + 2):
            if j == DEPTH + 1:
                pl.when(i == j)(lambda j=j: work(j % 3, j >= 3))
            for zz in range(DEPTH):
                pl.when((z == zz) & (i == j))(lambda zz=zz, j=j: talk(zz, j))
            if j < DEPTH + 1:
                pl.when(i == j)(lambda j=j: work(j % 3, j >= 3))
        return carry

    lax.fori_loop(0, DEPTH + 2, turn, 0)
    for k in range(3):
        give(k).wait_send()
    for zz in range(DEPTH):
        pl.when(z == zz)(lambda zz=zz: finish(zz))


def scatter_sums(part, xrows, row_grad, hidden, gate_grad, up_grad):
    blocks, rows, width = part.shape
    half, ff = width // 2, hidden.shape[1] // 2
    dtype = part.dtype
    vmem = pl.BlockSpec(memory_space=pltpu.VMEM)
    lots = [(width, ff), (width, ff), (ff, width)]
    held = [
        (2, DEPTH, rows, half),
        (2, DEPTH, rows, half),
        (2, 2, DEPTH, rows, half),
        (DEPTH, rows, width),
        (DEPTH + 1, rows, width),
    ]
    return pl.pallas_call(
        scatter_kernel,
        out_shape=tuple(jax.ShapeDtypeStruct(shape, dtype) for shape in [(rows, width), *lots]),
        in_specs=[vmem] * 6,
        out_specs=(vmem,) * 4,
        scratch_shapes=[pltpu.VMEM(shape, dtype) for shape in held + lots + lots]
        + [
            pltpu.SemaphoreType.DMA((DEPTH, 7)),
            pltpu.SemaphoreType.DMA((2, DEPTH)),
            pltpu.SemaphoreType.DMA((2, 2, DEPTH)),
            pltpu.SemaphoreType.DMA((DEPTH + 1,)),
            pltpu.SemaphoreType.DMA((3,)),
            pltpu.SemaphoreType.DMA((3,)),
        ],
        compiler_params=pltpu.CompilerParams(
            collective_id=1, has_side_effects=True, vmem_limit_bytes=58 * 1024 * 1024
        ),
    )(part, xrows, row_grad, hidden, gate_grad, up_grad)


def dequant(weight, scale):
    rows, cols = weight.shape
    srows, scols = scale.shape
    blocks = weight.reshape(srows, rows // srows, scols, cols // scols).astype(jnp.float32)
    return (blocks * scale[:, None, :, None]).reshape(rows, cols).astype(jnp.bfloat16)


def shards(
    x_quant, x_scale, out_grad, expert_ids, gate_fixed, w_gate, s_gate, w_up, s_up, w_down, s_down
):
    f32, bf16 = jnp.float32, jnp.bfloat16
    tok_rows, width = x_quant.shape
    topk = expert_ids.shape[1]
    experts = lax.axis_size("expert")
    capacity = tok_rows * topk * 5 // (4 * experts)
    blk_width = width // x_scale.shape[1]
    scaled = x_quant.reshape(tok_rows, -1, blk_width).astype(f32) * x_scale[:, :, None]
    inputs = scaled.reshape(tok_rows, width).astype(bf16)
    named = expert_ids[None, :, :] == jnp.arange(experts, dtype=jnp.int32)[:, None, None]
    units = jnp.sum(jnp.where(named, gate_fixed[None], 0), axis=2).astype(f32)
    units = lax.all_to_all(units, "expert", split_axis=0, concat_axis=0, tiled=True)

    chosen = units > 0
    rank = jnp.cumsum(chosen.astype(jnp.int32), axis=1) - 1
    pick = chosen[:, None, :] & (
        rank[:, None, :] == jnp.arange(capacity, dtype=jnp.int32)[None, :, None]
    )
    gates = jnp.sum(jnp.where(pick, units[:, None, :], 0.0), axis=2) / 65536.0
    pick = pick.astype(bf16)

    if experts == 4 * DEPTH:
        moved = routed_rows(
            inputs,
            out_grad,
            pick,
            pick.swapaxes(1, 2),
            gates[:, :, None],
            [w_gate[0], w_up[0], w_down[0]],
            [s_gate[0], s_up[0], s_down[0]],
        )
        grad_input, sum_gate, sum_up, sum_down = scatter_sums(*moved)
        return (grad_input, sum_gate[None], sum_up[None], sum_down[None])

    gate_w = dequant(w_gate[0], s_gate[0])
    up_w = dequant(w_up[0], s_up[0])
    down_w = dequant(w_down[0], s_down[0])
    rows = experts * capacity
    all_x = lax.all_gather(inputs, "expert", axis=0, tiled=False)
    all_g = lax.all_gather(out_grad, "expert", axis=0, tiled=False)
    xrows = jnp.einsum("ect,etd->ecd", pick, all_x, preferred_element_type=f32)
    xrows = xrows.astype(bf16).reshape(rows, width)
    row_grad = jnp.einsum("ect,etd->ecd", pick, all_g, preferred_element_type=f32)
    row_grad = (row_grad * gates[:, :, None]).astype(bf16).reshape(rows, width)
    pre_gate = jnp.dot(xrows, gate_w, preferred_element_type=f32)
    pre_up = jnp.dot(xrows, up_w, preferred_element_type=f32)
    sig = jax.nn.sigmoid(pre_gate)
    act = pre_gate * sig
    hidden = (act * pre_up).astype(bf16)
    hidden_grad = jnp.dot(row_grad, down_w.T, preferred_element_type=f32)
    up_grad = (hidden_grad * act).astype(bf16)
    gate_grad = (hidden_grad * pre_up * sig * (1.0 + pre_gate * (1.0 - sig))).astype(bf16)
    row_input = jnp.dot(gate_grad, gate_w.T, preferred_element_type=f32)
    row_input = row_input + jnp.dot(up_grad, up_w.T, preferred_element_type=f32)
    back = row_input.astype(bf16).reshape(experts, capacity, width)
    spread = jnp.einsum("ect,ecd->etd", pick, back, preferred_element_type=f32).astype(bf16)
    grad_input = lax.psum_scatter(
        spread.reshape(experts * tok_rows, width), "expert", scatter_dimension=0, tiled=True
    )
    term_gate = jnp.dot(xrows.T, gate_grad, preferred_element_type=f32).astype(bf16)
    term_up = jnp.dot(xrows.T, up_grad, preferred_element_type=f32).astype(bf16)
    term_down = jnp.dot(hidden.T, row_grad, preferred_element_type=f32).astype(bf16)
    sum_gate = lax.psum_scatter(term_gate, "replica", scatter_dimension=1, tiled=True)
    sum_up = lax.psum_scatter(term_up, "replica", scatter_dimension=1, tiled=True)
    sum_down = lax.psum_scatter(term_down, "replica", scatter_dimension=0, tiled=True)
    return (grad_input, sum_gate[None], sum_up[None], sum_down[None])


def solution(mesh):
    tokens = P(("expert", "replica"), None)
    weights = P("expert", None, None)
    return jax.shard_map(
        shards,
        mesh=mesh,
        in_specs=(tokens,) * 5 + (weights,) * 6,
        out_specs=(
            tokens,
            P("expert", None, "replica"),
            P("expert", None, "replica"),
            P("expert", "replica", None),
        ),
        check_vma=False,
    )
```
